256 devices in a mesh: rows: 32 (over x, z), cols: 8 (over y, core).
Axes of the slice: x: 4, y: 4, z: 8, core: 2. Of those that a mesh axis runs over, the one named last changes fastest.
Arguments:
- integrals: bfloat16 [32, 16, 64, 24576], P(None, None, 'rows', 'cols'), may hold values from -6 to 6
- density: bfloat16 [2048, 2048], P('cols', 'rows'), may hold values from -0.1875 to 0.1875
- neighbours: int32 [32, 16], replicated, may hold values from 0 to 31, all different within a row
- live: int32 [32], replicated, may hold values from 2 to 16, as said below
- sizes: int32 [32], replicated, may hold values from 48 to 64, as said below
Outputs:
- contracted: bfloat16 [32, 16, 64, 24576], P('rows', None, None, 'cols')
The draws below stay inside these ranges and needn't reach their ends.
Inputs may be any that keep to these rules, and one draw needn't show every extreme that they name: `neighbours`: each row names 16 different blocks; every block is named by some row. Some block has all 16 slots live. `sizes`: some block has 64 functions.
All inputs are finite; a program needn't handle non-finite values.
Results may differ from the reference program's by a relative error of at most 0.001.
Values may be sent and summed in bfloat16 or wider, within the bound.
A program may use at most 128 MiB of HBM per device.

```python
import jax
import jax.numpy as jnp
from jax import lax

BS = 64
NBLK = 32
NNB = 16
NP = 384
NF = 2048


def draw_live(key, part):
    key = jax.random.fold_in(key, 11)
    first_key, second_key = jax.random.split(key)
    counts = jax.random.randint(first_key, (NBLK,), 2, NNB + 1)
    where_full = jax.random.randint(second_key, (), 0, NBLK)
    return counts.at[where_full].set(NNB).astype(jnp.int32)


def draw_sizes(key, part):
    key = jax.random.fold_in(key, 23)
    first_key, second_key = jax.random.split(key)
    counts = jax.random.randint(first_key, (NBLK,), BS - BS // 4, BS + 1)
    where_full = jax.random.randint(second_key, (), 0, NBLK)
    return counts.at[where_full].set(BS).astype(jnp.int32)


def shard_levels(rng, extent, shards, least, high):
    def one(axis_at, parts):
        steps = jax.random.uniform(jax.random.fold_in(jax.random.fold_in(rng, 6), axis_at), (parts,), jnp.float32, least / len(shards), high / len(shards))
        return jnp.repeat(jnp.exp(steps), extent[axis_at] // parts).reshape((-1,) + (1,) * (len(extent) - axis_at - 1))

    loudness = one(*shards[0])
    for cut in shards[1:]:
        loudness = loudness * one(*cut)
    return loudness


def choose_distinct(key, rows, number_of, top, lift):
    sequence = jax.random.permutation(jax.random.fold_in(key, 1), number_of)
    favour = sequence
    for power in range(3):
        favour = favour * favour // number_of
    favour = favour * lift // number_of
    tickets = jax.random.randint(jax.random.fold_in(key, 2), (rows, number_of), 0, 4096) + favour
    holders = jax.random.permutation(jax.random.fold_in(key, 3), rows)[jnp.arange(number_of) % rows]
    tickets = jnp.where(jnp.arange(rows)[:, None] == holders[None, :], 1 << 14, tickets)
    score = tickets * number_of + jnp.arange(number_of)
    return lax.top_k(score.astype(jnp.int32), top)[1].astype(jnp.int32)


def bell_draw(key, extent, deviation, limit, cuts=(), kind=jnp.bfloat16):
    drawn = jax.random.normal(key, extent, jnp.float32) * deviation
    if len(cuts) > 0:
        drawn = shard_levels(key, extent, cuts, -0.22, 0.18) * drawn
    return jnp.clip(drawn, min=-limit, max=limit).astype(kind)


def setup_inputs(seed: int = 0) -> dict:
    key_of = jax.random.split(jax.random.key(seed), 6)
    return {
        "integrals": bell_draw(key_of[0], (NBLK, NNB, BS, NP * BS), 1.0, 6.0, ((2, 32), (3, 8))),
        "density": bell_draw(key_of[1], (NF, NF), (NNB * BS) ** -0.5, 0.1875, ((0, 8), (1, 32))),
        "neighbours": choose_distinct(key_of[2], NBLK, NBLK, NNB, 0),
        "live": draw_live(jax.random.fold_in(key_of[5], 71), 0),
        "sizes": draw_sizes(jax.random.fold_in(key_of[5], 71), 0),
    }


def reference(integrals, density, neighbours, live, sizes):
    slot_index = jnp.arange(NNB * BS, dtype=jnp.int32) // BS
    inner_index = jnp.arange(NNB * BS, dtype=jnp.int32) % BS
    column_index = jnp.arange(NP * BS, dtype=jnp.int32) % BS

    def per_block(block):
        partners = neighbours[block][slot_index]
        positions = partners * BS + inner_index
        usable = ((slot_index < live[block]) & (inner_index < sizes[partners])).astype(jnp.bfloat16)
        selected = density[positions][:, positions] * usable[:, None] * usable[None, :]
        keep = (column_index < sizes[block]).astype(jnp.bfloat16)
        masked = integrals[block].reshape(NNB * BS, NP * BS) * keep[None, :]
        result = jnp.dot(selected.T, masked, preferred_element_type=jnp.float32)
        return result.astype(jnp.bfloat16).reshape(NNB, BS, NP * BS)

    return lax.map(per_block, jnp.arange(NBLK, dtype=jnp.int32))
```

```python
import functools

import jax
import jax.numpy as jnp
from jax import lax
from jax.experimental import pallas as pl
from jax.experimental.pallas import tpu as pltpu
from jax.sharding import PartitionSpec as P

BS = 64
NX, NZ, NC = 4, 8, 8
NR = NX * NZ
MESH = pl.DeviceIdType.MESH


def exchange(x_ref, d_ref, neigh, live, sizes, r_ref, sel_ref, d1, mine, d2, xs, xr, zs, zr, qs, qr, ys, yr, local):
    row = lax.axis_index("rows")
    col = lax.axis_index("cols")
    x, z = row // NZ, row % NZ
    slots = neigh.shape[1]

    def at(dx, dz):
        return lax.rem(x + dx, NX) * NZ + lax.rem(z + dz, NZ)

    offsets = [(dx, dz) for dz in range(NZ) for dx in range(NX) if (dx, dz) != (0, 0)]
    barrier = pltpu.get_barrier_semaphore()
    for dx, dz in offsets:
        pl.semaphore_signal(barrier, inc=1, device_id=(at(dx, dz), col), device_id_type=MESH)
    for dc in range(1, NC):
        pl.semaphore_signal(barrier, inc=1, device_id=(row, lax.rem(col + dc, NC)), device_id_type=MESH)
    own = pltpu.make_async_copy(d_ref, d1.at[row], local.at[0])
    own.start()
    own_x = pltpu.make_async_copy(x_ref.at[row], r_ref.at[:, :, row], local.at[1])
    own_x.start()
    pl.semaphore_wait(barrier, len(offsets) + NC - 1)

    zcopies = []
    for i, dz in enumerate(range(1, NZ)):
        cp = pltpu.make_async_remote_copy(
            src_ref=d_ref, dst_ref=d1.at[row], send_sem=zs.at[i], recv_sem=zr.at[i],
            device_id=(at(0, dz), col), device_id_type=MESH)
        cp.start()
        zcopies.append(cp)
    copies = []
    for i, (dx, dz) in enumerate(offsets):
        to = at(dx, dz)
        cp = pltpu.make_async_remote_copy(
            src_ref=x_ref.at[to], dst_ref=r_ref.at[:, :, row], send_sem=xs.at[i], recv_sem=xr.at[i],
            device_id=(to, col), device_id_type=MESH)
        cp.start()
        copies.append(cp)

    own.wait()
    for cp in zcopies:
        cp.wait()
    xcopies = []
    for i, dx in enumerate(range(1, NX)):
        cp = pltpu.make_async_remote_copy(
            src_ref=d1.at[pl.ds(x * NZ, NZ)], dst_ref=d1.at[pl.ds(x * NZ, NZ)], send_sem=qs.at[i], recv_sem=qr.at[i],
            device_id=(at(dx, 0), col), device_id_type=MESH)
        cp.start()
        xcopies.append(cp)
    for cp in xcopies:
        cp.wait()

    inner = lax.broadcasted_iota(jnp.int32, (BS, 256), 0)
    for k in range(slots):
        other = neigh[row, k]
        limit = jnp.where(k < live[row], sizes[other], 0)
        mine[pl.ds(k * BS, BS), :] = jnp.where(inner < limit, d1[other], jnp.zeros((), jnp.bfloat16))

    ycopies = []
    for i, dc in enumerate(range(1, NC)):
        cp = pltpu.make_async_remote_copy(
            src_ref=mine, dst_ref=d2.at[col], send_sem=ys.at[i], recv_sem=yr.at[i],
            device_id=(row, lax.rem(col + dc, NC)), device_id_type=MESH)
        cp.start()
        ycopies.append(cp)
    d2[col] = mine[...]
    for cp in ycopies:
        cp.wait()

    wide = slots * BS
    lane = lax.broadcasted_iota(jnp.int32, (1, wide), 1)
    position = jnp.full((1, wide), -1, jnp.int32)
    for k in range(slots):
        other = neigh[row, k]
        limit = jnp.where(k < live[row], sizes[other], 0)
        here = (lane >= k * BS) & (lane < k * BS + limit)
        position = jnp.where(here, other * BS + lane - k * BS, position)

    @pl.loop(0, wide // 256)
    def _(part):
        rows_here = pl.ds(pl.multiple_of(part * 256, 256), 256)
        total = jnp.zeros((256, wide), jnp.float32)
        for c in range(NC):
            index = lax.broadcasted_iota(jnp.int32, (256, wide), 0) + c * 256
            pick = jnp.where(index == position, 1.0, 0.0).astype(jnp.bfloat16)
            total = total + jnp.dot(d2[c, rows_here, :], pick, preferred_element_type=jnp.float32)
        sel_ref[rows_here, :] = total.astype(jnp.bfloat16)

    own_x.wait()
    for cp in copies:
        cp.wait()


def contract(tiles, sizes, sel_ref, r_ref, o_ref):
    size = sizes[lax.axis_index("rows")]
    lane = lax.broadcasted_iota(jnp.int32, (1, 128), 1)
    keep = lax.rem(lane, BS) < size
    for pair in range(tiles // 2):
        rhs = jnp.concatenate(
            [r_ref[:, 2 * pair + h].reshape(r_ref.shape[0] * BS, 128) for h in range(2)], axis=1)
        out = jnp.dot(sel_ref[...], rhs, preferred_element_type=jnp.float32)
        for h in range(2):
            part = jnp.where(keep, out[:, h * 128:(h + 1) * 128], 0.0).astype(jnp.bfloat16)
            lanes = pl.ds((2 * pair + h) * 128, 128)
            o_ref[0, :, :, lanes] = part.reshape(r_ref.shape[0], BS, 128)


def shards(integrals, density, neighbours, live, sizes):
    blocks, slots, rows_each, width = integrals.shape
    lanes = width // 128
    view = integrals.reshape(blocks, slots, rows_each, lanes, 128).transpose(0, 1, 3, 2, 4)
    dma = pltpu.SemaphoreType.DMA
    smem = pl.BlockSpec(memory_space=pltpu.SMEM)
    anywhere = pl.BlockSpec(memory_space=pl.ANY)
    vmem = pl.BlockSpec(memory_space=pltpu.VMEM)
    wide = slots * BS
    received, selected = pl.pallas_call(
        exchange,
        out_shape=(
            jax.ShapeDtypeStruct((slots, lanes, blocks, rows_each, 128), jnp.bfloat16),
            jax.ShapeDtypeStruct((wide, wide), jnp.bfloat16),
        ),
        in_specs=[anywhere, vmem, smem, smem, smem],
        out_specs=(anywhere, vmem),
        scratch_shapes=[
            pltpu.VMEM((NR, BS, 256), jnp.bfloat16),
            pltpu.VMEM((wide, 256), jnp.bfloat16),
            pltpu.VMEM((NC, wide, 256), jnp.bfloat16),
            dma((NR - 1,)), dma((NR - 1,)),
            dma((NZ - 1,)), dma((NZ - 1,)),
            dma((NX - 1,)), dma((NX - 1,)),
            dma((NC - 1,)), dma((NC - 1,)),
            dma((2,)),
        ],
        compiler_params=pltpu.CompilerParams(
            collective_id=0, has_side_effects=True, vmem_limit_bytes=40 * 2**20),
        name="exchange",
    )(view, density.T, neighbours, live, sizes)
    flat = received.reshape(slots, lanes, blocks * rows_each, 128)
    tiles = 4
    return pl.pallas_call(
        functools.partial(contract, tiles),
        grid=(lanes // tiles,),
        in_specs=[
            smem,
            pl.BlockSpec((wide, wide), lambda i: (0, 0)),
            pl.BlockSpec((slots, tiles, BS, 128), lambda i: (0, i, 0, 0)),
        ],
        out_specs=pl.BlockSpec((1, slots, BS, tiles * 128), lambda i: (0, 0, 0, i)),
        out_shape=jax.ShapeDtypeStruct((1, slots, BS, width), jnp.bfloat16),
        compiler_params=pltpu.CompilerParams(vmem_limit_bytes=40 * 2**20),
        name="contract",
    )(sizes, selected, flat)


def solution(mesh):
    return jax.shard_map(
        shards,
        mesh=mesh,
        in_specs=(P(None, None, "rows", "cols"), P("cols", "rows"), P(), P(), P()),
        out_specs=P("rows", None, None, "cols"),
        check_vma=False,
    )
```

```python
import functools

import jax
import jax.numpy as jnp
from jax import lax
from jax.experimental import pallas as pl
from jax.experimental.pallas import tpu as pltpu
from jax.sharding import PartitionSpec as P

BS = 64
NX, NZ, NC = 4, 8, 8
NR = NX * NZ
MESH = pl.DeviceIdType.MESH
CHUNKS = (3, 5, 5, 4, 3, 2, 1, 1)
FIRST = tuple(sum(CHUNKS[:i]) for i in range(len(CHUNKS)))
AHEAD = 2
ZSTEPS = (4, 3, 5, 2, 6, 1, 7)
XSTEPS = (2, 1, 3)
CAPACITIES = tuple(range(36, 65, 4))


def exchange(capacity, x_ref, d_ref, table, neigh, live, sizes, r_ref, sel_ref, d1, mine, d2, *rest):
    n = len(CHUNKS)
    x_in, z_send, z_recv, x_send = (rest[i * n:(i + 1) * n] for i in range(4))
    in_sem, zss, zrs, xss, xrs, own_sem, zs, zr, qs, qr, ys, yr, dsem = rest[4 * n:]
    row = lax.axis_index("rows")
    col = lax.axis_index("cols")
    x, z = row // NZ, lax.rem(row, NZ)
    slots = neigh.shape[1]
    units = NX * slots

    def at(dx, dz):
        return lax.rem(x + dx, NX) * NZ + lax.rem(z + dz, NZ)

    loads = []
    for c in range(n):
        cp = pltpu.make_async_copy(x_ref.at[:, pl.ds(FIRST[c], CHUNKS[c])], x_in[c], in_sem.at[c])
        cp.start()
        loads.append(cp)
    own_d = pltpu.make_async_copy(d_ref, d1.at[row], dsem)
    own_d.start()

    barrier = pltpu.get_barrier_semaphore()
    for dz in ZSTEPS:
        pl.semaphore_signal(barrier, inc=1, device_id=(at(0, dz), col), device_id_type=MESH)
    for dx in XSTEPS:
        pl.semaphore_signal(barrier, inc=1, device_id=(at(dx, 0), col), device_id_type=MESH)
    for dc in range(1, NC):
        pl.semaphore_signal(barrier, inc=1, device_id=(row, lax.rem(col + dc, NC)), device_id_type=MESH)
    pl.semaphore_wait(barrier, NZ + NX + NC - 3)

    def pack(c):
        loads[c].wait()

        @pl.loop(0, capacity)
        def _(s):
            z_recv[c][z, s] = x_in[c][table[z, s]]
            for i, dz in enumerate(ZSTEPS):
                z_send[c][i, s] = x_in[c][table[lax.rem(z + dz, NZ), s]]

    def send_z(c):
        out = []
        for i, dz in enumerate(ZSTEPS):
            cp = pltpu.make_async_remote_copy(
                src_ref=z_send[c].at[i], dst_ref=z_recv[c].at[z], send_sem=zss.at[c, i], recv_sem=zrs.at[c, i],
                device_id=(at(0, dz), col), device_id_type=MESH)
            cp.start()
            out.append(cp)
        return out

    def unpack(c):
        @pl.loop(0, units)
        def _(p):
            place = table[NZ + z, p]
            for other in range(NZ):
                x_send[c][p, :, other] = z_recv[c][other, place]

    def send_x(c):
        out = []
        lanes = pl.ds(FIRST[c], CHUNKS[c])
        for i, dx in enumerate(XSTEPS):
            xp = lax.rem(x + dx, NX)
            cp = pltpu.make_async_remote_copy(
                src_ref=x_send[c].at[pl.ds(xp * slots, slots)], dst_ref=r_ref.at[:, lanes, pl.ds(x * NZ, NZ)],
                send_sem=xss.at[c, i], recv_sem=xrs.at[c, i],
                device_id=(at(dx, 0), col), device_id_type=MESH)
            cp.start()
            out.append(cp)
        cp = pltpu.make_async_copy(
            x_send[c].at[pl.ds(x * slots, slots)], r_ref.at[:, lanes, pl.ds(x * NZ, NZ)], own_sem.at[c])
        cp.start()
        out.append(cp)
        return out

    d_copies = []
    for i, dz in enumerate(ZSTEPS):
        cp = pltpu.make_async_remote_copy(
            src_ref=d_ref, dst_ref=d1.at[row], send_sem=zs.at[i], recv_sem=zr.at[i],
            device_id=(at(0, dz), col), device_id_type=MESH)
        cp.start()
        d_copies.append(cp)

    z_copies, x_copies = [], []
    for c in range(AHEAD):
        pack(c)
        z_copies.append(send_z(c))
    own_d.wait()
    for cp in d_copies:
        cp.wait()
    d_copies = []
    for i, dx in enumerate(XSTEPS):
        cp = pltpu.make_async_remote_copy(
            src_ref=d1.at[pl.ds(x * NZ, NZ)], dst_ref=d1.at[pl.ds(x * NZ, NZ)], send_sem=qs.at[i], recv_sem=qr.at[i],
            device_id=(at(dx, 0), col), device_id_type=MESH)
        cp.start()
        d_copies.append(cp)
    for c in range(AHEAD, n):
        pack(c)

    def density_rows():
        for cp in d_copies:
            cp.wait()
        inner = lax.broadcasted_iota(jnp.int32, (BS, 256), 0)
        for k in range(slots):
            other = neigh[row, k]
            limit = jnp.where(k < live[row], sizes[other], 0)
            mine[pl.ds(k * BS, BS), :] = jnp.where(inner < limit, d1[other], jnp.zeros((), jnp.bfloat16))
        out = []
        for i, dc in enumerate(range(1, NC)):
            cp = pltpu.make_async_remote_copy(
                src_ref=mine, dst_ref=d2.at[col], send_sem=ys.at[i], recv_sem=yr.at[i],
                device_id=(row, lax.rem(col + dc, NC)), device_id_type=MESH)
            cp.start()
            out.append(cp)
        d2[col] = mine[...]
        return out

    def density_columns():
        wide = slots * BS
        lane = lax.broadcasted_iota(jnp.int32, (1, wide), 1)
        position = jnp.full((1, wide), -1, jnp.int32)
        for k in range(slots):
            other = neigh[row, k]
            limit = jnp.where(k < live[row], sizes[other], 0)
            here = (lane >= k * BS) & (lane < k * BS + limit)
            position = jnp.where(here, other * BS + lane - k * BS, position)

        @pl.loop(0, wide // 256)
        def _(part):
            rows_here = pl.ds(pl.multiple_of(part * 256, 256), 256)
            total = jnp.zeros((256, wide), jnp.float32)
            for c in range(NC):
                index = lax.broadcasted_iota(jnp.int32, (256, wide), 0) + c * 256
                pick = jnp.where(index == position, 1.0, 0.0).astype(jnp.bfloat16)
                total = total + jnp.dot(d2[c, rows_here, :], pick, preferred_element_type=jnp.float32)
            sel_ref[rows_here, :] = total.astype(jnp.bfloat16)

    for c in range(n):
        for cp in z_copies[c]:
            cp.wait()
        if c + AHEAD < n:
            z_copies.append(send_z(c + AHEAD))
        unpack(c)
        x_copies += send_x(c)
        if c == 0:
            d_copies = density_rows()
        if c == 4:
            for cp in d_copies:
                cp.wait()
            density_columns()
    for cp in x_copies:
        cp.wait()


def contract(tiles, sizes, sel_ref, r_ref, o_ref):
    size = sizes[lax.axis_index("rows")]
    lane = lax.broadcasted_iota(jnp.int32, (1, 128), 1)
    keep = lax.rem(lane, BS) < size
    for pair in range(tiles // 2):
        rhs = jnp.concatenate(
            [r_ref[:, 2 * pair + h].reshape(r_ref.shape[0] * BS, 128) for h in range(2)], axis=1)
        out = jnp.dot(sel_ref[...], rhs, preferred_element_type=jnp.float32)
        for h in range(2):
            part = jnp.where(keep, out[:, h * 128:(h + 1) * 128], 0.0).astype(jnp.bfloat16)
            lanes = pl.ds((2 * pair + h) * 128, 128)
            o_ref[0, :, :, lanes] = part.reshape(r_ref.shape[0], BS, 128)


def tables(live, slots):
    counts = live.reshape(NX, NZ)
    ends = [counts[0]]
    for i in range(1, NX):
        ends.append(ends[-1] + counts[i])
    starts = [jnp.zeros_like(ends[0])] + ends[:-1]
    place = jnp.arange(NX * slots, dtype=jnp.int32)[None, :]
    target = jnp.arange(NZ, dtype=jnp.int32)[:, None]
    unit = jnp.zeros((NZ, NX * slots), jnp.int32)
    back = jnp.zeros((NZ, NX * slots), jnp.int32)
    for i in range(NX):
        start, end = starts[i][:, None], ends[i][:, None]
        unit = jnp.where((place >= start) & (place < end), (i * NZ + target) * slots + place - start, unit)
        slot = jnp.minimum(place - i * slots, end - start - 1)
        back = jnp.where((place >= i * slots) & (place < (i + 1) * slots), start + jnp.maximum(slot, 0), back)
    return jnp.concatenate([unit, back], axis=0), jnp.max(ends[-1])


def shards(integrals, density, neighbours, live, sizes):
    blocks, slots, rows_each, width = integrals.shape
    lanes = width // 128
    view = integrals.reshape(blocks * slots, rows_each, lanes, 128).transpose(0, 2, 1, 3)
    dma = pltpu.SemaphoreType.DMA
    smem = pl.BlockSpec(memory_space=pltpu.SMEM)
    anywhere = pl.BlockSpec(memory_space=pl.ANY)
    vmem = pl.BlockSpec(memory_space=pltpu.VMEM)
    wide = slots * BS
    n = len(CHUNKS)
    table, most = tables(live, slots)

    def call(which, capacity, *operands):
        def buffers(*lead):
            return [pltpu.VMEM(lead + (q, rows_each, 128), jnp.bfloat16) for q in CHUNKS]

        return pl.pallas_call(
            functools.partial(exchange, capacity),
            out_shape=(
                jax.ShapeDtypeStruct((slots, lanes, blocks, rows_each, 128), jnp.bfloat16),
                jax.ShapeDtypeStruct((wide, wide), jnp.bfloat16),
            ),
            in_specs=[anywhere, vmem, smem, smem, smem, smem],
            out_specs=(anywhere, vmem),
            scratch_shapes=[
                pltpu.VMEM((NR, BS, 256), jnp.bfloat16),
                pltpu.VMEM((wide, 256), jnp.bfloat16),
                pltpu.VMEM((NC, wide, 256), jnp.bfloat16),
                *buffers(blocks * slots), *buffers(NZ - 1, capacity), *buffers(NZ, capacity),
                *[pltpu.VMEM((NX * slots, q, NZ, rows_each, 128), jnp.bfloat16) for q in CHUNKS],
                dma((n,)),
                dma((n, NZ - 1)), dma((n, NZ - 1)),
                dma((n, NX - 1)), dma((n, NX - 1)),
                dma((n,)),
                dma((NZ - 1,)), dma((NZ - 1,)),
                dma((NX - 1,)), dma((NX - 1,)),
                dma((NC - 1,)), dma((NC - 1,)),
                dma,
            ],
            compiler_params=pltpu.CompilerParams(
                collective_id=which, has_side_effects=True, vmem_limit_bytes=56 * 2**20),
            name="exchange",
        )(*operands)

    which = jnp.clip((most - CAPACITIES[0] + 3) // 4, 0, len(CAPACITIES) - 1)
    received, selected = lax.switch(
        which, [functools.partial(call, i, capacity) for i, capacity in enumerate(CAPACITIES)],
        view, density.T, table, neighbours, live, sizes)
    flat = received.reshape(slots, lanes, blocks * rows_each, 128)
    tiles = 4
    return pl.pallas_call(
        functools.partial(contract, tiles),
        grid=(lanes // tiles,),
        in_specs=[
            smem,
            pl.BlockSpec((wide, wide), lambda i: (0, 0)),
            pl.BlockSpec((slots, tiles, BS, 128), lambda i: (0, i, 0, 0)),
        ],
        out_specs=pl.BlockSpec((1, slots, BS, tiles * 128), lambda i: (0, 0, 0, i)),
        out_shape=jax.ShapeDtypeStruct((1, slots, BS, width), jnp.bfloat16),
        compiler_params=pltpu.CompilerParams(vmem_limit_bytes=40 * 2**20),
        name="contract",
    )(sizes, selected, flat)


def solution(mesh):
    return jax.shard_map(
        shards,
        mesh=mesh,
        in_specs=(P(None, None, "rows", "cols"), P("cols", "rows"), P(), P(), P()),
        out_specs=P("rows", None, None, "cols"),
        check_vma=False,
    )
```

```python
import functools

import jax
import jax.numpy as jnp
from jax import lax
from jax.experimental import pallas as pl
from jax.experimental.pallas import tpu as pltpu
from jax.sharding import PartitionSpec as P

BS = 64
NX, NZ, NC = 4, 8, 8
NR = NX * NZ
MESH = pl.DeviceIdType.MESH
CHUNKS = (3, 5, 5, 4, 3, 2, 1, 1)
FIRST = tuple(sum(CHUNKS[:i]) for i in range(len(CHUNKS)))
AHEAD = 4
READY = 3
ZSTEPS = (4, 3, 5, 2, 6, 1, 7)
XSTEPS = (2, 1, 3)
CAPACITIES = tuple(range(36, 65, 2))


def exchange(capacity, x_ref, d_ref, table, neigh, live, sizes, y_ref, d1, mine, d2, sel, *rest):
    n = len(CHUNKS)
    x_in, z_send, z_recv, x_send, ready, stage = (rest[i * n:(i + 1) * n] for i in range(6))
    in_sem, zss, zrs, xss, xrs, own_sem, out_sem, zs, zr, qs, qr, ys, yr, dsem = rest[6 * n:]
    row = lax.axis_index("rows")
    col = lax.axis_index("cols")
    x, z = row // NZ, lax.rem(row, NZ)
    slots = neigh.shape[0]
    units = NX * slots

    def at(dx, dz):
        return lax.rem(x + dx, NX) * NZ + lax.rem(z + dz, NZ)

    loads = []
    for c in range(n):
        cp = pltpu.make_async_copy(x_ref.at[:, pl.ds(FIRST[c], CHUNKS[c])], x_in[c], in_sem.at[c])
        cp.start()
        loads.append(cp)
    own_d = pltpu.make_async_copy(d_ref, d1.at[row], dsem)
    own_d.start()

    barrier = pltpu.get_barrier_semaphore()
    for dz in ZSTEPS:
        pl.semaphore_signal(barrier, inc=1, device_id=(at(0, dz), col), device_id_type=MESH)
    for dx in XSTEPS:
        pl.semaphore_signal(barrier, inc=1, device_id=(at(dx, 0), col), device_id_type=MESH)
    for dc in range(1, NC):
        pl.semaphore_signal(barrier, inc=1, device_id=(row, lax.rem(col + dc, NC)), device_id_type=MESH)
    pl.semaphore_wait(barrier, NZ + NX + NC - 3)

    def pack(c):
        loads[c].wait()

        @pl.loop(0, capacity)
        def _(s):
            z_recv[c][z, s] = x_in[c][table[z, s]]
            for i, dz in enumerate(ZSTEPS):
                z_send[c][i, s] = x_in[c][table[lax.rem(z + dz, NZ), s]]

    def send_z(c):
        out = []
        for i, dz in enumerate(ZSTEPS):
            cp = pltpu.make_async_remote_copy(
                src_ref=z_send[c].at[i], dst_ref=z_recv[c].at[z], send_sem=zss.at[c, i], recv_sem=zrs.at[c, i],
                device_id=(at(0, dz), col), device_id_type=MESH)
            cp.start()
            out.append(cp)
        return out

    def unpack(c):
        @pl.loop(0, units)
        def _(p):
            place = table[NZ + z, p]
            for other in range(NZ):
                for j in range(CHUNKS[c]):
                    x_send[c][p, j, 2 * other:2 * other + 2, :] = z_recv[c][other, place, j]

    def send_x(c):
        out = []
        here = ready[c].at[:, :, pl.ds(pl.multiple_of(x * 16, 16), 16)]
        for i, dx in enumerate(XSTEPS):
            xp = lax.rem(x + dx, NX)
            cp = pltpu.make_async_remote_copy(
                src_ref=x_send[c].at[pl.ds(xp * slots, slots)], dst_ref=here,
                send_sem=xss.at[c, i], recv_sem=xrs.at[c, i],
                device_id=(at(dx, 0), col), device_id_type=MESH)
            cp.start()
            out.append(cp)
        cp = pltpu.make_async_copy(x_send[c].at[pl.ds(x * slots, slots)], here, own_sem.at[c])
        cp.start()
        out.append(cp)
        return out

    d_copies = []
    for i, dz in enumerate(ZSTEPS):
        cp = pltpu.make_async_remote_copy(
            src_ref=d_ref, dst_ref=d1.at[row], send_sem=zs.at[i], recv_sem=zr.at[i],
            device_id=(at(0, dz), col), device_id_type=MESH)
        cp.start()
        d_copies.append(cp)

    z_copies, x_copies = [], []
    for c in range(AHEAD):
        pack(c)
        z_copies.append(send_z(c))
    own_d.wait()
    for cp in d_copies:
        cp.wait()
    d_copies = []
    for i, dx in enumerate(XSTEPS):
        cp = pltpu.make_async_remote_copy(
            src_ref=d1.at[pl.ds(x * NZ, NZ)], dst_ref=d1.at[pl.ds(x * NZ, NZ)], send_sem=qs.at[i], recv_sem=qr.at[i],
            device_id=(at(dx, 0), col), device_id_type=MESH)
        cp.start()
        d_copies.append(cp)
    for c in range(AHEAD, n):
        pack(c)

    def density_rows():
        for cp in d_copies:
            cp.wait()
        inner = lax.broadcasted_iota(jnp.int32, (BS, 256), 0)
        for k in range(slots):
            other = neigh[k, row]
            limit = jnp.where(k < live[row], sizes[other], 0)
            mine[pl.ds(k * BS, BS), :] = jnp.where(inner < limit, d1[other], jnp.zeros((), jnp.bfloat16))
        out = []
        for i, dc in enumerate(range(1, NC)):
            cp = pltpu.make_async_remote_copy(
                src_ref=mine, dst_ref=d2.at[col], send_sem=ys.at[i], recv_sem=yr.at[i],
                device_id=(row, lax.rem(col + dc, NC)), device_id_type=MESH)
            cp.start()
            out.append(cp)
        d2[col] = mine[...]
        return out

    def density_columns():
        wide = slots * BS
        lane = lax.broadcasted_iota(jnp.int32, (1, wide), 1)
        position = jnp.full((1, wide), -1, jnp.int32)
        for k in range(slots):
            other = neigh[k, row]
            limit = jnp.where(k < live[row], sizes[other], 0)
            here = (lane >= k * BS) & (lane < k * BS + limit)
            position = jnp.where(here, other * BS + lane - k * BS, position)

        @pl.loop(0, wide // 256)
        def _(part):
            rows_here = pl.ds(pl.multiple_of(part * 256, 256), 256)
            total = jnp.zeros((256, wide), jnp.float32)
            for c in range(NC):
                index = lax.broadcasted_iota(jnp.int32, (256, wide), 0) + c * 256
                pick = jnp.where(index == position, 1.0, 0.0).astype(jnp.bfloat16)
                total = total + jnp.dot(d2[c, rows_here, :], pick, preferred_element_type=jnp.float32)
            sel[rows_here, :] = total.astype(jnp.bfloat16)

    size = sizes[row]
    keep = lax.rem(lax.broadcasted_iota(jnp.int32, (1, 128), 1), BS) < size

    def multiply(c):
        for cp in x_copies[c]:
            cp.wait()

        @pl.loop(0, slots // 4)
        def _(part):
            left = sel[pl.ds(pl.multiple_of(part * 4 * BS, 4 * BS), 4 * BS), :]
            for j in range(0, CHUNKS[c], 2):
                tiles = range(j, min(j + 2, CHUNKS[c]))
                right = jnp.concatenate([ready[c][:, t].reshape(slots * BS, 128) for t in tiles], axis=1)
                out = jnp.dot(left, right, preferred_element_type=jnp.float32)
                for h, t in enumerate(tiles):
                    tile = jnp.where(keep, out[:, h * 128:(h + 1) * 128], 0.0).astype(jnp.bfloat16)
                    stage[c][pl.ds(part * 4, 4), :, t * 128:(t + 1) * 128] = tile.reshape(4, BS, 128)

        cp = pltpu.make_async_copy(
            stage[c], y_ref.at[0, :, :, pl.ds(FIRST[c] * 128, CHUNKS[c] * 128)], out_sem.at[c])
        cp.start()
        return cp

    stores = []
    for c in range(n):
        for cp in z_copies[c]:
            cp.wait()
        if c + AHEAD < n:
            z_copies.append(send_z(c + AHEAD))
        unpack(c)
        x_copies.append(send_x(c))
        if c == 0:
            d_copies = density_rows()
        if c == READY:
            for cp in d_copies:
                cp.wait()
            density_columns()
        if c > READY:
            for _ in range(2):
                if len(stores) < c - 1:
                    stores.append(multiply(len(stores)))
    while len(stores) < n:
        stores.append(multiply(len(stores)))
    for cp in stores:
        cp.wait()


def tables(live, slots):
    counts = live.reshape(NX, NZ)
    ends = [counts[0]]
    for i in range(1, NX):
        ends.append(ends[-1] + counts[i])
    starts = [jnp.zeros_like(ends[0])] + ends[:-1]
    place = jnp.arange(NX * slots, dtype=jnp.int32)[None, :]
    target = jnp.arange(NZ, dtype=jnp.int32)[:, None]
    unit = jnp.zeros((NZ, NX * slots), jnp.int32)
    back = jnp.zeros((NZ, NX * slots), jnp.int32)
    for i in range(NX):
        start, end = starts[i][:, None], ends[i][:, None]
        unit = jnp.where((place >= start) & (place < end), (i * NZ + target) * slots + place - start, unit)
        slot = jnp.minimum(place - i * slots, end - start - 1)
        back = jnp.where((place >= i * slots) & (place < (i + 1) * slots), start + jnp.maximum(slot, 0), back)
    return jnp.concatenate([unit, back], axis=0), jnp.max(ends[-1])


def shards(integrals, density, neighbours, live, sizes):
    blocks, slots, rows_each, width = integrals.shape
    lanes = width // 128
    view = integrals.reshape(blocks * slots, rows_each, lanes, 128).transpose(0, 2, 1, 3)
    dma = pltpu.SemaphoreType.DMA
    smem = pl.BlockSpec(memory_space=pltpu.SMEM)
    anywhere = pl.BlockSpec(memory_space=pl.ANY)
    vmem = pl.BlockSpec(memory_space=pltpu.VMEM)
    wide = slots * BS
    n = len(CHUNKS)
    table, most = tables(live, slots)

    def call(which, capacity, *operands):
        def buffers(*lead):
            return [pltpu.VMEM(lead + (q, rows_each, 128), jnp.bfloat16) for q in CHUNKS]

        return pl.pallas_call(
            functools.partial(exchange, capacity),
            out_shape=jax.ShapeDtypeStruct((1, slots, BS, width), jnp.bfloat16),
            in_specs=[anywhere, vmem, smem, smem, smem, smem],
            out_specs=anywhere,
            scratch_shapes=[
                pltpu.VMEM((NR, BS, 256), jnp.bfloat16),
                pltpu.VMEM((wide, 256), jnp.bfloat16),
                pltpu.VMEM((NC, wide, 256), jnp.bfloat16),
                pltpu.VMEM((wide, wide), jnp.bfloat16),
                *buffers(blocks * slots), *buffers(NZ - 1, capacity), *buffers(NZ, capacity),
                *[pltpu.VMEM((NX * slots, q, NZ * rows_each, 128), jnp.bfloat16) for q in CHUNKS],
                *[pltpu.VMEM((slots, q, BS, 128), jnp.bfloat16) for q in CHUNKS],
                *[pltpu.VMEM((slots, BS, q * 128), jnp.bfloat16) for q in CHUNKS],
                dma((n,)),
                dma((n, NZ - 1)), dma((n, NZ - 1)),
                dma((n, NX - 1)), dma((n, NX - 1)),
                dma((n,)), dma((n,)),
                dma((NZ - 1,)), dma((NZ - 1,)),
                dma((NX - 1,)), dma((NX - 1,)),
                dma((NC - 1,)), dma((NC - 1,)),
                dma,
            ],
            compiler_params=pltpu.CompilerParams(
                collective_id=which, has_side_effects=True, vmem_limit_bytes=48 * 2**20),
            name="exchange",
        )(*operands)

    which = jnp.clip((most - CAPACITIES[0] + 1) // 2, 0, len(CAPACITIES) - 1)
    return lax.switch(
        which, [functools.partial(call, i, capacity) for i, capacity in enumerate(CAPACITIES)],
        view, density.T, table, neighbours.T, live, sizes)


def solution(mesh):
    return jax.shard_map(
        shards,
        mesh=mesh,
        in_specs=(P(None, None, "rows", "cols"), P("cols", "rows"), P(), P(), P()),
        out_specs=P("rows", None, None, "cols"),
        check_vma=False,
    )
```

```python
import functools

import jax
import jax.numpy as jnp
from jax import lax
from jax.experimental import pallas as pl
from jax.experimental.pallas import tpu as pltpu
from jax.sharding import PartitionSpec as P

BS = 64
NX, NZ, NC = 4, 8, 8
NR = NX * NZ
MESH = pl.DeviceIdType.MESH
CHUNKS = (4, 4, 6, 4, 2, 2, 1, 1)
FIRST = tuple(sum(CHUNKS[:i]) for i in range(len(CHUNKS)))
AHEAD = 4
READY = 3
MULTIPLY = {READY + 1: ((0, 1),), READY + 2: ((2,),), READY + 3: ((3, 4),), READY + 4: ((5,), (6, 7))}
CAPACITIES = (44, 46, 48, 50, 52, 54, 58, 64)


def exchange(capacity, x_ref, d_ref, table, neigh, live, sizes, y_ref, d1, mine, d2, sel, ready, stage, *rest):
    n = len(CHUNKS)
    x_in, z_send, z_recv, x_send = (rest[i * n:(i + 1) * n] for i in range(4))
    in_sem, out_sem, zss, zrs, zos, xss, xrs, xos, dzs, dzr, dxs, dxr, dys, dyr, dsem = rest[4 * n:]
    row = lax.axis_index("rows")
    col = lax.axis_index("cols")
    x, z = row // NZ, lax.rem(row, NZ)
    slots = neigh.shape[0]
    units = NX * slots
    wide = slots * BS

    def at(dx, dz):
        return lax.rem(x + dx, NX) * NZ + lax.rem(z + dz, NZ)

    def far_first(i):
        return 4 + (i // 2) * (1 - lax.rem(i, 2)) - ((i + 1) // 2) * lax.rem(i, 2)

    def load(c):
        return pltpu.make_async_copy(x_ref.at[:, pl.ds(FIRST[c], CHUNKS[c])], x_in[c], in_sem.at[c])

    def each(count, copy, act):
        @pl.loop(0, count)
        def _(i):
            act(copy(i))

    def start(cp):
        cp.start()

    def wait(cp):
        cp.wait()

    def z_copy(c, i):
        dz = far_first(i)
        return pltpu.make_async_remote_copy(
            src_ref=z_send[c].at[dz], dst_ref=z_recv[c].at[z], send_sem=zss.at[c, i], recv_sem=zrs.at[c, i],
            device_id=(at(0, dz), col), device_id_type=MESH)

    def z_own(c):
        return pltpu.make_async_copy(z_send[c].at[0], z_recv[c].at[z], zos.at[c])

    def landing(c):
        return ready.at[pl.ds(FIRST[c], CHUNKS[c]), :, pl.ds(pl.multiple_of(x * 16, 16), 16)]

    def x_copy(c, i):
        dx = i + 1
        return pltpu.make_async_remote_copy(
            src_ref=x_send[c].at[lax.rem(x + dx, NX)], dst_ref=landing(c), send_sem=xss.at[c, i], recv_sem=xrs.at[c, i],
            device_id=(at(dx, 0), col), device_id_type=MESH)

    def x_own(c):
        return pltpu.make_async_copy(x_send[c].at[x], landing(c), xos.at[c])

    def dz_copy(i):
        return pltpu.make_async_remote_copy(
            src_ref=d_ref, dst_ref=d1.at[row], send_sem=dzs.at[i], recv_sem=dzr.at[i],
            device_id=(at(0, i + 1), col), device_id_type=MESH)

    def dx_copy(i):
        here = d1.at[pl.ds(x * NZ, NZ)]
        return pltpu.make_async_remote_copy(
            src_ref=here, dst_ref=here, send_sem=dxs.at[i], recv_sem=dxr.at[i],
            device_id=(at(i + 1, 0), col), device_id_type=MESH)

    def dy_copy(i):
        return pltpu.make_async_remote_copy(
            src_ref=mine, dst_ref=d2.at[col], send_sem=dys.at[i], recv_sem=dyr.at[i],
            device_id=(row, lax.rem(col + i + 1, NC)), device_id_type=MESH)

    for c in range(n):
        load(c).start()
    own_d = pltpu.make_async_copy(d_ref, d1.at[row], dsem)
    own_d.start()

    barrier = pltpu.get_barrier_semaphore()
    for dz in range(1, NZ):
        pl.semaphore_signal(barrier, inc=1, device_id=(at(0, dz), col), device_id_type=MESH)
    for dx in range(1, NX):
        pl.semaphore_signal(barrier, inc=1, device_id=(at(dx, 0), col), device_id_type=MESH)
    for dc in range(1, NC):
        pl.semaphore_signal(barrier, inc=1, device_id=(row, lax.rem(col + dc, NC)), device_id_type=MESH)
    pl.semaphore_wait(barrier, NZ + NX + NC - 3)

    def pack(c):
        load(c).wait()

        @pl.loop(0, capacity)
        def _(s):
            for dz in range(NZ):
                z_send[c][dz, s] = x_in[c][table[lax.rem(z + dz, NZ), s]]

    def send_z(c):
        each(NZ - 1, functools.partial(z_copy, c), start)
        z_own(c).start()

    def unpack(c):
        @pl.loop(0, units)
        def _(p):
            place = table[NZ + z, p]
            for other in range(NZ):
                for j in range(CHUNKS[c]):
                    x_send[c][p // slots, j, lax.rem(p, slots), 2 * other:2 * other + 2, :] = z_recv[c][other, place, j]

    each(NZ - 1, dz_copy, start)
    for c in range(AHEAD):
        pack(c)
        send_z(c)
    own_d.wait()
    each(NZ - 1, dz_copy, wait)
    each(NX - 1, dx_copy, start)
    for c in range(AHEAD, n):
        pack(c)

    def limit_of(k):
        return jnp.where(k < live[row], sizes[neigh[k, row]], 0)

    def density_rows():
        each(NX - 1, dx_copy, wait)
        inner = lax.broadcasted_iota(jnp.int32, (BS, 256), 0)

        @pl.loop(0, slots)
        def _(k):
            mine[pl.ds(pl.multiple_of(k * BS, BS), BS), :] = jnp.where(
                inner < limit_of(k), d1[neigh[k, row]], jnp.zeros((), jnp.bfloat16))

        each(NC - 1, dy_copy, start)
        d2[col] = mine[...]

    def density_columns():
        each(NC - 1, dy_copy, wait)
        index = lax.broadcasted_iota(jnp.int32, (256, 128), 0)
        lane = lax.broadcasted_iota(jnp.int32, (256, 128), 1)

        @pl.loop(0, slots // 2)
        def _(pair):
            picks = []
            for h in range(2):
                other = neigh[2 * pair + h, row]
                here = (lane >= h * BS) & (lane < h * BS + limit_of(2 * pair + h))
                hit = here & (index == lax.rem(other, 4) * BS + lane - h * BS)
                picks.append((other // 4, jnp.where(hit, 1.0, 0.0).astype(jnp.bfloat16)))

            @pl.loop(0, wide // 256)
            def _(part):
                rows_here = pl.ds(pl.multiple_of(part * 256, 256), 256)
                total = sum(jnp.dot(d2[c, rows_here, :], pick, preferred_element_type=jnp.float32) for c, pick in picks)
                sel[rows_here, pl.ds(pl.multiple_of(pair * 128, 128), 128)] = total.astype(jnp.bfloat16)

    keep = lax.rem(lax.broadcasted_iota(jnp.int32, (1, 256), 1), BS) < sizes[row]

    def multiply(chunks):
        for c in chunks:
            each(NX - 1, functools.partial(x_copy, c), wait)
            x_own(c).wait()

        first, last = FIRST[chunks[0]], FIRST[chunks[-1]] + CHUNKS[chunks[-1]]

        @pl.loop(0, (last - first) // 2)
        def _(pair):
            t = first + 2 * pair
            right = jnp.concatenate([ready[t].reshape(wide, 128), ready[t + 1].reshape(wide, 128)], axis=1)

            @pl.loop(0, slots // 4)
            def _(part):
                left = sel[pl.ds(pl.multiple_of(part * 256, 256), 256), :]
                out = jnp.dot(left, right, preferred_element_type=jnp.float32)
                tile = jnp.where(keep, out, 0.0).astype(jnp.bfloat16)
                stage[pl.ds(part * 4, 4), :, pl.ds(pl.multiple_of(t * 128, 256), 256)] = tile.reshape(4, BS, 256)

        cp = pltpu.make_async_copy(
            stage.at[:, :, pl.ds(first * 128, (last - first) * 128)],
            y_ref.at[0, :, :, pl.ds(first * 128, (last - first) * 128)], out_sem.at[chunks[0]])
        cp.start()
        return cp

    stores = []
    for c in range(n):
        each(NZ - 1, functools.partial(z_copy, c), wait)
        z_own(c).wait()
        if c + AHEAD < n:
            send_z(c + AHEAD)
        unpack(c)
        each(NX - 1, functools.partial(x_copy, c), start)
        x_own(c).start()
        if c == 0:
            density_rows()
        if c == READY:
            density_columns()
        if c in MULTIPLY:
            stores += [multiply(chunks) for chunks in MULTIPLY[c]]
    for cp in stores:
        cp.wait()


def tables(live, slots):
    counts = live.reshape(NX, NZ)
    ends = [counts[0]]
    for i in range(1, NX):
        ends.append(ends[-1] + counts[i])
    starts = [jnp.zeros_like(ends[0])] + ends[:-1]
    place = jnp.arange(NX * slots, dtype=jnp.int32)[None, :]
    target = jnp.arange(NZ, dtype=jnp.int32)[:, None]
    unit = jnp.zeros((NZ, NX * slots), jnp.int32)
    back = jnp.zeros((NZ, NX * slots), jnp.int32)
    for i in range(NX):
        start, end = starts[i][:, None], ends[i][:, None]
        unit = jnp.where((place >= start) & (place < end), (i * NZ + target) * slots + place - start, unit)
        slot = jnp.minimum(place - i * slots, end - start - 1)
        back = jnp.where((place >= i * slots) & (place < (i + 1) * slots), start + jnp.maximum(slot, 0), back)
    return jnp.concatenate([unit, back], axis=0), jnp.max(ends[-1])


def shards(integrals, density, neighbours, live, sizes):
    blocks, slots, rows_each, width = integrals.shape
    lanes = width // 128
    view = integrals.reshape(blocks * slots, rows_each, lanes, 128).transpose(0, 2, 1, 3)
    dma = pltpu.SemaphoreType.DMA
    smem = pl.BlockSpec(memory_space=pltpu.SMEM)
    anywhere = pl.BlockSpec(memory_space=pl.ANY)
    vmem = pl.BlockSpec(memory_space=pltpu.VMEM)
    wide = slots * BS
    n = len(CHUNKS)
    table, most = tables(live, slots)

    def call(which, capacity, *operands):
        def buffers(*lead):
            return [pltpu.VMEM(lead + (q, rows_each, 128), jnp.bfloat16) for q in CHUNKS]

        return pl.pallas_call(
            functools.partial(exchange, capacity),
            out_shape=jax.ShapeDtypeStruct((1, slots, BS, width), jnp.bfloat16),
            in_specs=[anywhere, vmem, smem, smem, smem, smem],
            out_specs=anywhere,
            scratch_shapes=[
                pltpu.VMEM((NR, BS, 256), jnp.bfloat16),
                pltpu.VMEM((wide, 256), jnp.bfloat16),
                pltpu.VMEM((NC, wide, 256), jnp.bfloat16),
                pltpu.VMEM((wide, wide), jnp.bfloat16),
                pltpu.VMEM((lanes, slots, BS, 128), jnp.bfloat16),
                pltpu.VMEM((slots, BS, width), jnp.bfloat16),
                *buffers(blocks * slots), *buffers(NZ, capacity), *buffers(NZ, capacity),
                *[pltpu.VMEM((NX, q, slots, NZ * rows_each, 128), jnp.bfloat16) for q in CHUNKS],
                dma((n,)), dma((n,)),
                dma((n, NZ - 1)), dma((n, NZ - 1)), dma((n,)),
                dma((n, NX - 1)), dma((n, NX - 1)), dma((n,)),
                dma((NZ - 1,)), dma((NZ - 1,)),
                dma((NX - 1,)), dma((NX - 1,)),
                dma((NC - 1,)), dma((NC - 1,)),
                dma,
            ],
            compiler_params=pltpu.CompilerParams(
                collective_id=which, has_side_effects=True, vmem_limit_bytes=48 * 2**20),
            name="exchange",
        )(*operands)

    which = sum((most > capacity).astype(jnp.int32) for capacity in CAPACITIES[:-1])
    return lax.switch(
        which, [functools.partial(call, i, capacity) for i, capacity in enumerate(CAPACITIES)],
        view, density.T, table, neighbours.T, live, sizes)


def solution(mesh):
    return jax.shard_map(
        shards,
        mesh=mesh,
        in_specs=(P(None, None, "rows", "cols"), P("cols", "rows"), P(), P(), P()),
        out_specs=P("rows", None, None, "cols"),
        check_vma=False,
    )
```

```python
import functools

import jax
import jax.numpy as jnp
from jax import lax
from jax.experimental import pallas as pl
from jax.experimental.pallas import tpu as pltpu
from jax.sharding import PartitionSpec as P

BS = 64
NX, NZ, NC = 4, 8, 8
NR = NX * NZ
MESH = pl.DeviceIdType.MESH
CHUNKS = (4, 4, 6, 4, 2, 2, 1, 1)
FIRST = tuple(sum(CHUNKS[:i]) for i in range(len(CHUNKS)))
AHEAD = 4
READY = 2
MULTIPLY = {3: ((0, 1),), 4: ((2,),), 5: ((3,),), 7: ((4, 5), (6, 7))}
CAPACITIES = (44, 46, 48, 50, 52, 54, 58, 64)


def exchange(capacity, x_ref, d_ref, table, neigh, live, sizes, y_ref, d1, mine, d2, sel, ready, stage, *rest):
    n = len(CHUNKS)
    x_in, z_send, z_recv, x_send = (rest[i * n:(i + 1) * n] for i in range(4))
    in_sem, out_sem, zss, zrs, zos, xss, xrs, xos, dzs, dzr, dxs, dxr, dys, dyr, dsem = rest[4 * n:]
    row = lax.axis_index("rows")
    col = lax.axis_index("cols")
    x, z = row // NZ, lax.rem(row, NZ)
    slots = neigh.shape[0]
    units = NX * slots
    wide = slots * BS

    def at(dx, dz):
        return lax.rem(x + dx, NX) * NZ + lax.rem(z + dz, NZ)

    def far_first(i):
        return 4 + (i // 2) * (1 - lax.rem(i, 2)) - ((i + 1) // 2) * lax.rem(i, 2)

    def load(c):
        return pltpu.make_async_copy(x_ref.at[:, pl.ds(FIRST[c], CHUNKS[c])], x_in[c], in_sem.at[c])

    def each(count, copy, act):
        @pl.loop(0, count)
        def _(i):
            act(copy(i))

    def start(cp):
        cp.start()

    def wait(cp):
        cp.wait()

    def z_copy(c, i):
        dz = far_first(i)
        return pltpu.make_async_remote_copy(
            src_ref=z_send[c].at[dz], dst_ref=z_recv[c].at[z], send_sem=zss.at[c, i], recv_sem=zrs.at[c, i],
            device_id=(at(0, dz), col), device_id_type=MESH)

    def z_own(c):
        return pltpu.make_async_copy(z_send[c].at[0], z_recv[c].at[z], zos.at[c])

    def landing(c):
        return ready.at[pl.ds(FIRST[c], CHUNKS[c]), :, pl.ds(pl.multiple_of(x * 16, 16), 16)]

    def x_copy(c, i):
        dx = i + 1
        return pltpu.make_async_remote_copy(
            src_ref=x_send[c].at[lax.rem(x + dx, NX)], dst_ref=landing(c), send_sem=xss.at[c, i], recv_sem=xrs.at[c, i],
            device_id=(at(dx, 0), col), device_id_type=MESH)

    def x_own(c):
        return pltpu.make_async_copy(x_send[c].at[x], landing(c), xos.at[c])

    def dz_copy(i):
        return pltpu.make_async_remote_copy(
            src_ref=d_ref, dst_ref=d1.at[row], send_sem=dzs.at[i], recv_sem=dzr.at[i],
            device_id=(at(0, i + 1), col), device_id_type=MESH)

    def dx_copy(i):
        here = d1.at[pl.ds(x * NZ, NZ)]
        return pltpu.make_async_remote_copy(
            src_ref=here, dst_ref=here, send_sem=dxs.at[i], recv_sem=dxr.at[i],
            device_id=(at(i + 1, 0), col), device_id_type=MESH)

    def dy_copy(i):
        return pltpu.make_async_remote_copy(
            src_ref=mine, dst_ref=d2.at[col], send_sem=dys.at[i], recv_sem=dyr.at[i],
            device_id=(row, lax.rem(col + i + 1, NC)), device_id_type=MESH)

    for c in range(n):
        load(c).start()
    own_d = pltpu.make_async_copy(d_ref, d1.at[row], dsem)
    own_d.start()

    barrier = pltpu.get_barrier_semaphore()
    for dz in range(1, NZ):
        pl.semaphore_signal(barrier, inc=1, device_id=(at(0, dz), col), device_id_type=MESH)
    for dx in range(1, NX):
        pl.semaphore_signal(barrier, inc=1, device_id=(at(dx, 0), col), device_id_type=MESH)
    for dc in range(1, NC):
        pl.semaphore_signal(barrier, inc=1, device_id=(row, lax.rem(col + dc, NC)), device_id_type=MESH)
    pl.semaphore_wait(barrier, NZ + NX + NC - 3)

    def pack(c):
        load(c).wait()

        @pl.loop(0, capacity)
        def _(s):
            for dz in range(NZ):
                z_send[c][dz, s] = x_in[c][table[lax.rem(z + dz, NZ), s]]

    def send_z(c):
        each(NZ - 1, functools.partial(z_copy, c), start)
        z_own(c).start()

    def unpack(c):
        @pl.loop(0, units)
        def _(p):
            place = table[NZ + z, p]
            for other in range(NZ):
                for j in range(CHUNKS[c]):
                    x_send[c][p // slots, j, lax.rem(p, slots), 2 * other:2 * other + 2, :] = z_recv[c][other, place, j]

    each(NZ - 1, dz_copy, start)
    for c in range(AHEAD):
        pack(c)
        send_z(c)
    own_d.wait()
    each(NZ - 1, dz_copy, wait)
    each(NX - 1, dx_copy, start)
    for c in range(AHEAD, n):
        pack(c)

    def limit_of(k):
        return jnp.where(k < live[row], sizes[neigh[k, row]], 0)

    def density_rows():
        each(NX - 1, dx_copy, wait)
        inner = lax.broadcasted_iota(jnp.int32, (BS, 256), 0)

        @pl.loop(0, slots)
        def _(k):
            mine[pl.ds(pl.multiple_of(k * BS, BS), BS), :] = jnp.where(
                inner < limit_of(k), d1[neigh[k, row]], jnp.zeros((), jnp.bfloat16))

        each(NC - 1, dy_copy, start)
        d2[col] = mine[...]

    density_rows()

    def density_columns():
        each(NC - 1, dy_copy, wait)
        index = lax.broadcasted_iota(jnp.int32, (256, 128), 0)
        lane = lax.broadcasted_iota(jnp.int32, (256, 128), 1)

        @pl.loop(0, slots // 2)
        def _(pair):
            picks = []
            for h in range(2):
                other = neigh[2 * pair + h, row]
                here = (lane >= h * BS) & (lane < h * BS + limit_of(2 * pair + h))
                hit = here & (index == lax.rem(other, 4) * BS + lane - h * BS)
                picks.append((other // 4, jnp.where(hit, 1.0, 0.0).astype(jnp.bfloat16)))

            @pl.loop(0, wide // 256)
            def _(part):
                rows_here = pl.ds(pl.multiple_of(part * 256, 256), 256)
                total = sum(jnp.dot(d2[c, rows_here, :], pick, preferred_element_type=jnp.float32) for c, pick in picks)
                sel[rows_here, pl.ds(pl.multiple_of(pair * 128, 128), 128)] = total.astype(jnp.bfloat16)

    keep = lax.rem(lax.broadcasted_iota(jnp.int32, (1, 256), 1), BS) < sizes[row]

    def multiply(chunks):
        for c in chunks:
            each(NX - 1, functools.partial(x_copy, c), wait)
            x_own(c).wait()

        first, last = FIRST[chunks[0]], FIRST[chunks[-1]] + CHUNKS[chunks[-1]]

        @pl.loop(0, (last - first) // 2)
        def _(pair):
            t = first + 2 * pair
            right = jnp.concatenate([ready[t].reshape(wide, 128), ready[t + 1].reshape(wide, 128)], axis=1)

            @pl.loop(0, slots // 4)
            def _(part):
                left = sel[pl.ds(pl.multiple_of(part * 256, 256), 256), :]
                out = jnp.dot(left, right, preferred_element_type=jnp.float32)
                tile = jnp.where(keep, out, 0.0).astype(jnp.bfloat16)
                stage[pl.ds(part * 4, 4), :, pl.ds(pl.multiple_of(t * 128, 256), 256)] = tile.reshape(4, BS, 256)

        cp = pltpu.make_async_copy(
            stage.at[:, :, pl.ds(first * 128, (last - first) * 128)],
            y_ref.at[0, :, :, pl.ds(first * 128, (last - first) * 128)], out_sem.at[chunks[0]])
        cp.start()
        return cp

    stores = []
    for c in range(n):
        each(NZ - 1, functools.partial(z_copy, c), wait)
        z_own(c).wait()
        if c + AHEAD < n:
            send_z(c + AHEAD)
        unpack(c)
        each(NX - 1, functools.partial(x_copy, c), start)
        x_own(c).start()
        if c == READY:
            density_columns()
        if c in MULTIPLY:
            stores += [multiply(chunks) for chunks in MULTIPLY[c]]
    for cp in stores:
        cp.wait()


def tables(live, slots):
    counts = live.reshape(NX, NZ)
    ends = [counts[0]]
    for i in range(1, NX):
        ends.append(ends[-1] + counts[i])
    starts = [jnp.zeros_like(ends[0])] + ends[:-1]
    place = jnp.arange(NX * slots, dtype=jnp.int32)[None, :]
    target = jnp.arange(NZ, dtype=jnp.int32)[:, None]
    unit = jnp.zeros((NZ, NX * slots), jnp.int32)
    back = jnp.zeros((NZ, NX * slots), jnp.int32)
    for i in range(NX):
        start, end = starts[i][:, None], ends[i][:, None]
        unit = jnp.where((place >= start) & (place < end), (i * NZ + target) * slots + place - start, unit)
        slot = jnp.minimum(place - i * slots, end - start - 1)
        back = jnp.where((place >= i * slots) & (place < (i + 1) * slots), start + jnp.maximum(slot, 0), back)
    over = sum((ends[-1] > capacity).astype(jnp.int32) for capacity in CAPACITIES[:-1])
    return jnp.concatenate([unit, back], axis=0), jnp.max(over)


def shards(integrals, density, neighbours, live, sizes):
    blocks, slots, rows_each, width = integrals.shape
    lanes = width // 128
    view = integrals.reshape(blocks * slots, rows_each, lanes, 128).transpose(0, 2, 1, 3)
    dma = pltpu.SemaphoreType.DMA
    smem = pl.BlockSpec(memory_space=pltpu.SMEM)
    anywhere = pl.BlockSpec(memory_space=pl.ANY)
    vmem = pl.BlockSpec(memory_space=pltpu.VMEM)
    wide = slots * BS
    n = len(CHUNKS)
    table, which = tables(live, slots)

    def call(which, capacity, *operands):
        def buffers(*lead):
            return [pltpu.VMEM(lead + (q, rows_each, 128), jnp.bfloat16) for q in CHUNKS]

        return pl.pallas_call(
            functools.partial(exchange, capacity),
            out_shape=jax.ShapeDtypeStruct((1, slots, BS, width), jnp.bfloat16),
            in_specs=[anywhere, vmem, smem, smem, smem, smem],
            out_specs=anywhere,
            scratch_shapes=[
                pltpu.VMEM((NR, BS, 256), jnp.bfloat16),
                pltpu.VMEM((wide, 256), jnp.bfloat16),
                pltpu.VMEM((NC, wide, 256), jnp.bfloat16),
                pltpu.VMEM((wide, wide), jnp.bfloat16),
                pltpu.VMEM((lanes, slots, BS, 128), jnp.bfloat16),
                pltpu.VMEM((slots, BS, width), jnp.bfloat16),
                *buffers(blocks * slots), *buffers(NZ, capacity), *buffers(NZ, capacity),
                *[pltpu.VMEM((NX, q, slots, NZ * rows_each, 128), jnp.bfloat16) for q in CHUNKS],
                dma((n,)), dma((n,)),
                dma((n, NZ - 1)), dma((n, NZ - 1)), dma((n,)),
                dma((n, NX - 1)), dma((n, NX - 1)), dma((n,)),
                dma((NZ - 1,)), dma((NZ - 1,)),
                dma((NX - 1,)), dma((NX - 1,)),
                dma((NC - 1,)), dma((NC - 1,)),
                dma,
            ],
            compiler_params=pltpu.CompilerParams(
                collective_id=which, has_side_effects=True, vmem_limit_bytes=48 * 2**20),
            name="exchange",
        )(*operands)

    return lax.switch(
        which, [functools.partial(call, i, capacity) for i, capacity in enumerate(CAPACITIES)],
        view, density.T, table, neighbours.T, live, sizes)


def solution(mesh):
    return jax.shard_map(
        shards,
        mesh=mesh,
        in_specs=(P(None, None, "rows", "cols"), P("cols", "rows"), P(), P(), P()),
        out_specs=P("rows", None, None, "cols"),
        check_vma=False,
    )
```
